256 devices in a mesh: vocab: 32 (over x, z), hid: 8 (over y, core).
Axes of the slice: x: 4, y: 4, z: 8, core: 2. Of those that a mesh axis runs over, the one named last changes fastest.
Arguments:
- student_hidden: bfloat16 [1024, 8192], P(None, 'hid'), as said below
- head_weight: bfloat16 [8192, 65536], P('hid', 'vocab'), as said below
- teacher_logits: bfloat16 [1024, 65536], P(('vocab', 'hid')), as said below
Outputs:
- loss_value: float32 [], replicated
- grad_hidden: bfloat16 [1024, 8192], P('vocab', 'hid')
- grad_weight: bfloat16 [8192, 65536], P('hid', 'vocab')
Inputs may be any that keep to these rules, and one draw needn't show every extreme that they name: `student_hidden`: hidden states of order one to some tens. `head_weight`: weights of order one over the square root of 8192. `teacher_logits`: logits of order one to some hundreds.
All inputs are finite; a program needn't handle non-finite values.
Results may differ from the reference program's by a relative error of at most 0.02055.
Values may be sent and summed in bfloat16 or wider, within the bound.
No kernel may reach another device: no remote copies, remote signals or barrier semaphores. Data moves between devices by JAX's collectives and lax.ppermute only.
A program may use at most 128 MiB of HBM per device.

```python
import jax
import jax.numpy as jnp
from jax import lax

D = 8192
TOKENS = 1024
V = 65536


def draw_head_weight(key, part):
    key = jax.random.fold_in(key, 11)
    weight = jax.random.normal(key, (D, V), jnp.float32) * D ** (-0.5)
    return weight.astype(jnp.bfloat16)


def draw_student_hidden(key, part):
    key = jax.random.fold_in(key, 12)
    hidden = 3.0 * jax.random.truncated_normal(key, -4.0, 4.0, (TOKENS, D), jnp.float32)
    return hidden.astype(jnp.bfloat16)


def draw_teacher_logits(key, part):
    key = jax.random.fold_in(key, 13)
    key_val = jax.random.fold_in(key, 0)
    logits = 3.0 * jax.random.truncated_normal(key_val, -4.0, 4.0, (TOKENS, V), jnp.float32)
    return logits.astype(jnp.bfloat16)


def setup_inputs(seed: int = 0) -> dict:
    key_of = jax.random.split(jax.random.key(seed), 4)
    student_hidden = draw_student_hidden(jax.random.fold_in(key_of[3], 71), 0)
    head_weight = draw_head_weight(jax.random.fold_in(key_of[3], 71), 0)
    teacher_logits = draw_teacher_logits(jax.random.fold_in(key_of[3], 71), 0)
    return dict(student_hidden=student_hidden, head_weight=head_weight, teacher_logits=teacher_logits)


def log_softmax_rows(values):
    top_value = jnp.max(values, axis=1, keepdims=True)
    total = jnp.sum(jnp.exp(values - top_value), axis=1, keepdims=True)
    return values - top_value - jnp.log(total)


def reference(student_hidden, head_weight, teacher_logits):
    logits = jnp.dot(student_hidden, head_weight, preferred_element_type=jnp.float32)
    student_log = log_softmax_rows(logits)
    teacher_log = log_softmax_rows(teacher_logits.astype(jnp.float32))
    probs = jnp.exp(student_log)
    log_ratio = student_log - teacher_log
    kl_row = jnp.sum(probs * log_ratio, axis=1, keepdims=True)
    loss_value = jnp.sum(kl_row) / TOKENS
    grad_logits = (probs * (log_ratio - kl_row) / TOKENS).astype(jnp.bfloat16)
    grad_hidden = lax.dot_general(grad_logits, head_weight, (((1,), (1,)), ((), ())), preferred_element_type=jnp.float32).astype(jnp.bfloat16)
    grad_weight = lax.dot_general(student_hidden, grad_logits, (((0,), (0,)), ((), ())), preferred_element_type=jnp.float32).astype(jnp.bfloat16)
    return (loss_value, grad_hidden, grad_weight)
```

```python
import jax
import jax.numpy as jnp
from jax import lax
from jax.sharding import PartitionSpec as P

BF16 = jnp.bfloat16
F32 = jnp.float32
NX, NZ, NY = 4, 8, 4


def to_core(a):
    return lax.ppermute(a, "hid", [(i, i ^ 1) for i in range(2 * NY)])


def to_y(a, d):
    return lax.ppermute(a, "hid", [(i, (i + 2 * d) % (2 * NY)) for i in range(2 * NY)])


def to_x(a, d):
    return lax.ppermute(a, "vocab", [(i, (i + NZ * d) % (NX * NZ)) for i in range(NX * NZ)])


def take(a, i):
    return lax.dynamic_index_in_dim(a, i, 0, keepdims=False)


def shards(student_hidden, head_weight, teacher_logits):
    n_vocab = NX * NZ
    tokens, depth = student_hidden.shape
    width = head_weight.shape[1]
    hid = lax.axis_index("hid")
    y, core = hid // 2, hid % 2
    x = lax.axis_index("vocab") // NZ
    rows = tokens // 8
    by_y = student_hidden.reshape(2, 16, NY, 8, depth)
    mine, other = take(by_y, core), take(by_y, 1 - core)

    def rows_of(part, d):
        return lax.dynamic_index_in_dim(part, (y + d) % NY, 1, keepdims=False).reshape(rows, depth)

    order = (2, 1, 3, 0)
    hid_other = jnp.concatenate([rows_of(other, d) for d in order])
    hid_mine = jnp.concatenate([rows_of(mine, d) for d in order])

    def dot(a):
        return jnp.dot(a, head_weight, preferred_element_type=F32)

    got_a = to_core(dot(hid_other[:rows]))
    got_b = to_core(dot(hid_other[rows:]))
    part = dot(hid_mine)
    u2 = part[:rows] + got_a
    half = rows // 2
    r1 = to_y(u2[:half], 1)
    r2 = to_y(u2[half:], -1)
    u1 = part[rows : 2 * rows] + got_b[:rows]
    u3 = part[2 * rows : 3 * rows] + got_b[rows : 2 * rows]
    u0 = part[3 * rows :] + got_b[2 * rows :]
    r3 = to_y(u1[half:], 1)
    r4 = to_y(u3[:half], -1)
    tiles = lax.all_to_all(teacher_logits, "vocab", split_axis=1, concat_axis=0, tiled=True)
    tiles = tiles.reshape(2, 16, 4, width)
    theirs = to_core(take(tiles, 1 - core))
    own = take(tiles, core)
    both = jnp.stack([own, theirs])
    teacher = jnp.stack([take(both, core), take(both, 1 - core)], axis=1).reshape(rows, width).astype(F32)
    r5 = to_y(u1[:half] + r1, 1)
    r6 = to_y(u3[half:] + r2, -1)
    logits = u0 + jnp.concatenate([r4 + r5, r3 + r6])

    m = jnp.max(logits, axis=1)
    mt = jnp.max(teacher, axis=1)
    ls = logits - m[:, None]
    lt = teacher - mt[:, None]
    e = jnp.exp(ls)
    s = jnp.sum(e, axis=1)
    st = jnp.sum(jnp.exp(lt), axis=1)
    cross = jnp.sum(e * (ls - lt), axis=1)
    terms = jnp.stack([m, s, mt, st, cross, m, m, m])
    terms = jnp.broadcast_to(terms[None], (n_vocab, 8, rows))
    terms = lax.all_to_all(terms, "vocab", split_axis=0, concat_axis=0, tiled=True)
    gm, gs, gmt, gst, gc = (terms[:, i] for i in range(5))
    top, top_t = jnp.max(gm, axis=0), jnp.max(gmt, axis=0)
    w = jnp.exp(gm - top)
    total = jnp.sum(gs * w, axis=0)
    total_t = jnp.sum(gst * jnp.exp(gmt - top_t), axis=0)
    log_total, log_total_t = jnp.log(total), jnp.log(total_t)
    mean_ratio = jnp.sum(w * (gc + gs * ((gm - top) - (gmt - top_t))), axis=0) / total
    kl_row = mean_ratio - log_total + log_total_t
    lse = top + log_total
    lse_t = top_t + log_total_t

    student_log = logits - lse[:, None]
    teacher_log = teacher - lse_t[:, None]
    probs = jnp.exp(student_log)
    grad = (probs * (student_log - teacher_log - kl_row[:, None]) / tokens).astype(BF16)

    g1, g2 = grad[:half], grad[half:]
    a1, a2 = to_y(g1, 1), to_y(g2, -1)
    own_b = to_core(grad)
    a3, a4 = to_y(g2, 1), to_y(g1, -1)
    a5, a6 = to_y(a1, 1), to_y(a2, -1)
    near = jnp.concatenate([a4, a2, a1, a3])
    far = jnp.concatenate([a5, a6])
    near_b = to_core(near)
    far_b = to_core(far)
    grads = jnp.concatenate([far, near, grad, far_b, near_b, own_b])
    hiddens = jnp.concatenate([hid_mine, hid_other])
    part_hidden = lax.dot_general(
        grads, head_weight, (((1,), (1,)), ((), ())), preferred_element_type=F32
    ).astype(BF16)
    part_hidden = part_hidden.reshape(2, NY, 2, NZ, 8, depth)

    def for_x(d):
        to = (x + d) % NX
        which = jnp.where(to // 2 == core, 0, 1)
        piece = lax.dynamic_slice(
            part_hidden, (which, 0, to % 2, 0, 0, 0), (1, NY, 1, NZ, 8, depth)
        )
        return piece.reshape(NY, NZ, 8, depth)

    got = [to_x(for_x(d), d) for d in (2, 1, 3)]
    summed = for_x(0).astype(F32)
    for g in got:
        summed = summed + g.astype(F32)
    summed = summed.astype(BF16).transpose(1, 0, 2, 3).reshape(NZ * NY * 8, depth)
    z_groups = [[i * NZ + j for j in range(NZ)] for i in range(NX)]
    pieces = lax.all_to_all(
        summed, "vocab", split_axis=0, concat_axis=0, tiled=True, axis_index_groups=z_groups
    )
    rel = jnp.sum(pieces.reshape(NZ, NY, 8, depth).astype(F32), axis=0).astype(BF16)
    at = {d: i for i, d in enumerate(order)}
    lookup = jnp.array([at[d] for d in range(NY)], jnp.int32)
    grad_hidden = jnp.concatenate(
        [take(rel, lookup[(i - y) % NY]) for i in range(NY)]
    )

    grad_weight = lax.dot_general(
        hiddens, grads, (((0,), (0,)), ((), ())), preferred_element_type=F32
    ).astype(BF16)

    loss = jnp.sum(kl_row)
    loss = loss + to_core(loss)
    loss = loss + to_y(loss, 2)
    loss = loss + to_y(loss, 1)
    return (loss / tokens, grad_hidden, grad_weight)


def solution(mesh):
    in_specs = (P(None, "hid"), P("hid", "vocab"), P(("vocab", "hid"), None))
    out_specs = (P(), P("vocab", "hid"), P("hid", "vocab"))
    return jax.shard_map(shards, mesh=mesh, in_specs=in_specs, out_specs=out_specs, check_vma=False)
```

```python
import jax
import jax.numpy as jnp
from jax import lax
from jax.sharding import PartitionSpec as P

BF16 = jnp.bfloat16
F32 = jnp.float32
NX, NZ, NY = 4, 8, 4
ORDER = (2, 1, 3, 0)


def to_core(a):
    return lax.ppermute(a, "hid", [(i, i ^ 1) for i in range(2 * NY)])


def to_y(a, d):
    return lax.ppermute(a, "hid", [(i, (i + 2 * d) % (2 * NY)) for i in range(2 * NY)])


def to_x(a, d):
    return lax.ppermute(a, "vocab", [(i, (i + NZ * d) % (NX * NZ)) for i in range(NX * NZ)])


def take(a, i):
    return lax.dynamic_index_in_dim(a, i, 0, keepdims=False)


def shards(student_hidden, head_weight, teacher_logits):
    n_vocab = NX * NZ
    tokens, depth = student_hidden.shape
    width = head_weight.shape[1]
    hid = lax.axis_index("hid")
    y, core = hid // 2, hid % 2
    x = lax.axis_index("vocab") // NZ
    rows = tokens // 8
    half = rows // 2

    def rows_of(hidden, part, *ds):
        by_part = take(hidden.reshape(2, 16, NY, 8, depth), core if part == 0 else 1 - core)
        return jnp.concatenate(
            [
                lax.dynamic_index_in_dim(by_part, (y + d) % NY, 1, keepdims=False).reshape(
                    rows, depth
                )
                for d in ds
            ]
        )

    def dot(a):
        return jnp.dot(a, head_weight, preferred_element_type=F32)

    def both_parts(*ds):
        return lax.optimization_barrier(
            (rows_of(student_hidden, 1, *ds), rows_of(student_hidden, 0, *ds))
        )

    h_far_b, h_far = both_parts(2)
    got = to_core(dot(h_far_b))
    far = dot(h_far) + got
    r1 = to_y(far[:half], 1)
    r2 = to_y(far[half:], -1)
    h_near_b, h_near = both_parts(1, 3)
    got = to_core(dot(h_near_b))
    near = dot(h_near) + got
    r3 = to_y(near[half:rows], 1)
    r4 = to_y(near[rows : rows + half], -1)
    h_own_b, h_own = both_parts(0)
    got = to_core(dot(h_own_b))
    own = dot(h_own) + got
    teacher_logits, hidden_again, _ = lax.optimization_barrier(
        (teacher_logits, student_hidden, near)
    )
    tiles = lax.all_to_all(teacher_logits, "vocab", split_axis=1, concat_axis=0, tiled=True)
    tiles = tiles.reshape(2, 16, 4, width)
    theirs = to_core(take(tiles, 1 - core))
    both = jnp.stack([take(tiles, core), theirs])
    teacher = jnp.stack([take(both, core), take(both, 1 - core)], axis=1).reshape(rows, width)
    hiddens = jnp.concatenate(
        [rows_of(hidden_again, 0, *ORDER), rows_of(hidden_again, 1, *ORDER)]
    ).T
    teacher, hiddens = lax.optimization_barrier((teacher, hiddens))
    teacher = teacher.astype(F32)

    r5 = to_y(near[:half] + r1, 1)
    r6 = to_y(near[rows + half :] + r2, -1)
    logits = own + jnp.concatenate([r4 + r5, r3 + r6])

    m = jnp.max(logits, axis=1)
    mt = jnp.max(teacher, axis=1)
    ls = logits - m[:, None]
    lt = teacher - mt[:, None]
    e = jnp.exp(ls)
    s = jnp.sum(e, axis=1)
    st = jnp.sum(jnp.exp(lt), axis=1)
    cross = jnp.sum(e * (ls - lt), axis=1)
    terms = jnp.stack([m, s, mt, st, cross, m, m, m])
    terms = jnp.broadcast_to(terms[None], (n_vocab, 8, rows))
    terms = lax.all_to_all(terms, "vocab", split_axis=0, concat_axis=0, tiled=True)
    gm, gs, gmt, gst, gc = (terms[:, i] for i in range(5))
    top, top_t = jnp.max(gm, axis=0), jnp.max(gmt, axis=0)
    w = jnp.exp(gm - top)
    total = jnp.sum(gs * w, axis=0)
    total_t = jnp.sum(gst * jnp.exp(gmt - top_t), axis=0)
    log_total, log_total_t = jnp.log(total), jnp.log(total_t)
    mean_ratio = jnp.sum(w * (gc + gs * ((gm - top) - (gmt - top_t))), axis=0) / total
    kl_row = mean_ratio - log_total + log_total_t
    lse = top + log_total
    lse_t = top_t + log_total_t

    student_log = logits - lse[:, None]
    teacher_log = teacher - lse_t[:, None]
    probs = jnp.exp(student_log)
    grad = (probs * (student_log - teacher_log - kl_row[:, None]) / tokens).astype(BF16)

    g1, g2 = grad[:half], grad[half:]
    a1, a2 = to_y(g1, 1), to_y(g2, -1)
    own_b = to_core(grad)
    a3, a4 = to_y(g2, 1), to_y(g1, -1)
    a5, a6 = to_y(a1, 1), to_y(a2, -1)
    near = jnp.concatenate([a4, a2, a1, a3])
    near_b = to_core(near)
    far = jnp.concatenate([a5, a6])
    far_b = to_core(far)

    grads = jnp.concatenate([far, near, grad, far_b, near_b, own_b])
    part_hidden = lax.dot_general(
        grads, head_weight, (((1,), (1,)), ((), ())), preferred_element_type=F32
    ).astype(BF16)
    part_hidden = part_hidden.reshape(2, NY, 2, NZ, 8, depth)

    def for_x(d):
        to = (x + d) % NX
        which = jnp.where(to // 2 == core, 0, 1)
        piece = lax.dynamic_slice(
            part_hidden, (which, 0, to % 2, 0, 0, 0), (1, NY, 1, NZ, 8, depth)
        )
        return piece.reshape(NY, NZ, 8, depth)

    def add(a, b):
        return (a.astype(F32) + b.astype(F32)).astype(BF16)

    p2, p1, p3 = for_x(2), for_x(1), for_x(3)
    q1, q2 = to_x(p2[:2], 1), to_x(p2[2:], -1)
    q3, q4 = to_x(p1[2:], 1), to_x(p3[:2], -1)
    q5, q6 = to_x(add(p1[:2], q1), 1), to_x(add(p3[2:], q2), -1)
    summed = for_x(0).astype(F32) + jnp.concatenate(
        [q4.astype(F32) + q5.astype(F32), q3.astype(F32) + q6.astype(F32)]
    )
    summed = summed.astype(BF16)
    grad_weight = jnp.dot(hiddens, grads, preferred_element_type=F32).astype(BF16)

    kl_sum = jnp.broadcast_to(jnp.sum(kl_row), (8, 128))
    kl_sum = kl_sum + to_core(kl_sum)
    summed, grad_weight, kl_sum = lax.optimization_barrier((summed, grad_weight, kl_sum))
    summed = summed.transpose(1, 0, 2, 3).reshape(NZ * NY * 8, depth)
    z_groups = [[i * NZ + j for j in range(NZ)] for i in range(NX)]
    pieces = lax.all_to_all(
        summed, "vocab", split_axis=0, concat_axis=0, tiled=True, axis_index_groups=z_groups
    )
    rel = jnp.sum(pieces.reshape(NZ, NY, 8, depth).astype(F32), axis=0).astype(BF16)
    def place(d):
        return jnp.where(d == 2, 0, jnp.where(d == 0, 3, jnp.where(d == 1, 1, 2)))

    grad_hidden = jnp.concatenate([take(rel, place((i - y) % NY)) for i in range(NY)])

    total = (kl_sum + to_y(kl_sum, 2)) + (to_y(kl_sum, 1) + to_y(kl_sum, -1))
    loss = total[0, 0]
    return (loss / tokens, grad_hidden, grad_weight)


def solution(mesh):
    in_specs = (P(None, "hid"), P("hid", "vocab"), P(("vocab", "hid"), None))
    out_specs = (P(), P("vocab", "hid"), P("hid", "vocab"))
    return jax.shard_map(shards, mesh=mesh, in_specs=in_specs, out_specs=out_specs, check_vma=False)
```

```python
import jax
import jax.numpy as jnp
from jax import lax
from jax.experimental import pallas as pl
from jax.experimental.pallas import tpu as pltpu
from jax.sharding import PartitionSpec as P

BF16 = jnp.bfloat16
F32 = jnp.float32
NX, NZ, NY = 4, 8, 4
ORDER = (2, 1, 3, 0)


def to_core(a):
    return lax.ppermute(a, "hid", [(i, i ^ 1) for i in range(2 * NY)])


def to_y(a, d):
    return lax.ppermute(a, "hid", [(i, (i + 2 * d) % (2 * NY)) for i in range(2 * NY)])


def to_x(a, d):
    return lax.ppermute(a, "vocab", [(i, (i + NZ * d) % (NX * NZ)) for i in range(NX * NZ)])


def take(a, i):
    return lax.dynamic_index_in_dim(a, i, 0, keepdims=False)


def terms_kernel(logits_a, logits_b, teacher_ref, out_ref):
    half = logits_a.shape[0]
    rows = 2 * half
    lane = lax.broadcasted_iota(jnp.int32, (half, 128), 1)

    def table(logits, teacher):
        m = jnp.max(logits, axis=1, keepdims=True)
        mt = jnp.max(teacher, axis=1, keepdims=True)
        ls = logits - m
        lt = teacher - mt
        e = jnp.exp(ls)
        s = jnp.sum(e, axis=1, keepdims=True)
        st = jnp.sum(jnp.exp(lt), axis=1, keepdims=True)
        cross = jnp.sum(e * (ls - lt), axis=1, keepdims=True)
        out = jnp.zeros((half, 128), F32)
        for i, column in enumerate((m, s, mt, st, cross)):
            out = jnp.where(lane == i, column, out)
        return out

    terms = jnp.concatenate(
        [
            table(logits_a[...], teacher_ref[:half].astype(F32)),
            table(logits_b[...], teacher_ref[half:].astype(F32)),
        ]
    ).T[:8]
    for i in range(out_ref.shape[0]):
        out_ref[i] = terms


def row_terms(logits_a, logits_b, teacher, copies):
    rows, width = teacher.shape
    return pl.pallas_call(
        terms_kernel,
        out_shape=jax.ShapeDtypeStruct((copies, 8, rows), F32),
        compiler_params=pltpu.CompilerParams(vmem_limit_bytes=24 * 2**20),
        cost_estimate=pl.CostEstimate(
            flops=12 * teacher.size,
            bytes_accessed=6 * teacher.size,
            transcendentals=2 * teacher.size,
        ),
    )(logits_a, logits_b, teacher)


def shards(student_hidden, head_weight, teacher_logits):
    n_vocab = NX * NZ
    tokens, depth = student_hidden.shape
    width = head_weight.shape[1]
    hid = lax.axis_index("hid")
    y, core = hid // 2, hid % 2
    x = lax.axis_index("vocab") // NZ
    rows = tokens // 8
    half = rows // 2

    def rows_of(hidden, part, *ds):
        by_part = take(hidden.reshape(2, 16, NY, 8, depth), core if part == 0 else 1 - core)
        return jnp.concatenate(
            [
                lax.dynamic_index_in_dim(by_part, (y + d) % NY, 1, keepdims=False).reshape(
                    rows, depth
                )
                for d in ds
            ]
        )

    def dot(a):
        return jnp.dot(a, head_weight, preferred_element_type=F32)

    def both_parts(*ds):
        return lax.optimization_barrier(
            (rows_of(student_hidden, 1, *ds), rows_of(student_hidden, 0, *ds))
        )

    h_far_b, h_far = both_parts(2)
    got = to_core(dot(h_far_b))
    far = dot(h_far) + got
    h_near_b, h_near = both_parts(1, 3)
    h_near_b, h_near, far = lax.optimization_barrier((h_near_b, h_near, far))
    r1 = to_y(far[:half], 1)
    r2 = to_y(far[half:], -1)
    got = to_core(dot(h_near_b))
    near = dot(h_near) + got
    r3 = to_y(near[half:rows], 1)
    r4 = to_y(near[rows : rows + half], -1)
    h_own_b, h_own = both_parts(0)
    h_own_b, h_own, near = lax.optimization_barrier((h_own_b, h_own, near))
    got = to_core(dot(h_own_b))
    own = dot(h_own) + got
    teacher_logits, _ = lax.optimization_barrier((teacher_logits, near))
    r1, r2, r3, r4, hidden_again = lax.optimization_barrier((r1, r2, r3, r4, student_hidden))
    tiles = lax.all_to_all(teacher_logits, "vocab", split_axis=1, concat_axis=0, tiled=True)
    tiles = tiles.reshape(2, 16, 4, width)
    theirs = to_core(take(tiles, 1 - core))
    both = jnp.stack([take(tiles, core), theirs])
    teacher = jnp.stack([take(both, core), take(both, 1 - core)], axis=1).reshape(rows, width)
    hiddens = jnp.concatenate(
        [rows_of(hidden_again, 0, *ORDER), rows_of(hidden_again, 1, *ORDER)]
    ).T
    teacher, hiddens = lax.optimization_barrier((teacher, hiddens))
    r5 = to_y(near[:half] + r1, 1)
    r6 = to_y(near[rows + half :] + r2, -1)
    logits = (own[:half] + (r4 + r5), own[half:] + (r3 + r6))

    terms = row_terms(*logits, teacher, n_vocab)
    terms = lax.all_to_all(terms, "vocab", split_axis=0, concat_axis=0, tiled=True)
    gm, gs, gmt, gst, gc = (terms[:, i] for i in range(5))
    top, top_t = jnp.max(gm, axis=0), jnp.max(gmt, axis=0)
    w = jnp.exp(gm - top)
    total = jnp.sum(gs * w, axis=0)
    total_t = jnp.sum(gst * jnp.exp(gmt - top_t), axis=0)
    log_total, log_total_t = jnp.log(total), jnp.log(total_t)
    mean_ratio = jnp.sum(w * (gc + gs * ((gm - top) - (gmt - top_t))), axis=0) / total
    kl_row = mean_ratio - log_total + log_total_t
    lse = top + log_total
    lse_t = top_t + log_total_t

    student_log = jnp.concatenate(logits) - lse[:, None]
    teacher_log = teacher.astype(F32) - lse_t[:, None]
    probs = jnp.exp(student_log)
    grad = (probs * (student_log - teacher_log - kl_row[:, None]) / tokens).astype(BF16)

    g1, g2 = grad[:half], grad[half:]
    a1, a2 = to_y(g1, 1), to_y(g2, -1)
    own_b = to_core(grad)
    a3, a4 = to_y(g2, 1), to_y(g1, -1)
    a5, a6 = to_y(a1, 1), to_y(a2, -1)
    near = jnp.concatenate([a4, a2, a1, a3])
    near_b = to_core(near)
    far = jnp.concatenate([a5, a6])
    far_b = to_core(far)

    grads = jnp.concatenate([far, near, grad, far_b, near_b, own_b])
    part_hidden = lax.dot_general(
        grads, head_weight, (((1,), (1,)), ((), ())), preferred_element_type=F32
    ).astype(BF16)
    part_hidden = part_hidden.reshape(2, NY, 2, NZ, 8, depth)

    def for_x(d):
        to = (x + d) % NX
        which = jnp.where(to // 2 == core, 0, 1)
        piece = lax.dynamic_slice(
            part_hidden, (which, 0, to % 2, 0, 0, 0), (1, NY, 1, NZ, 8, depth)
        )
        return piece.reshape(NY, NZ, 8, depth)

    def add(a, b):
        return (a.astype(F32) + b.astype(F32)).astype(BF16)

    p2, p1, p3 = for_x(2), for_x(1), for_x(3)
    q1, q2 = to_x(p2[:2], 1), to_x(p2[2:], -1)
    q3, q4 = to_x(p1[2:], 1), to_x(p3[:2], -1)
    q5, q6 = to_x(add(p1[:2], q1), 1), to_x(add(p3[2:], q2), -1)
    summed = for_x(0).astype(F32) + jnp.concatenate(
        [q4.astype(F32) + q5.astype(F32), q3.astype(F32) + q6.astype(F32)]
    )
    summed = summed.astype(BF16)
    grad_weight = jnp.dot(hiddens, grads, preferred_element_type=F32).astype(BF16)

    summed, grad_weight, kl_row = lax.optimization_barrier((summed, grad_weight, kl_row))
    kl_sum = jnp.broadcast_to(jnp.sum(kl_row), (8, 128))
    kl_sum = kl_sum + to_core(kl_sum)
    summed = summed.transpose(1, 0, 2, 3).reshape(NZ * NY * 8, depth)
    z_groups = [[i * NZ + j for j in range(NZ)] for i in range(NX)]
    pieces = lax.all_to_all(
        summed, "vocab", split_axis=0, concat_axis=0, tiled=True, axis_index_groups=z_groups
    )
    rel = jnp.sum(pieces.reshape(NZ, NY, 8, depth).astype(F32), axis=0).astype(BF16)
    def place(d):
        return jnp.where(d == 2, 0, jnp.where(d == 0, 3, jnp.where(d == 1, 1, 2)))

    grad_hidden = jnp.concatenate([take(rel, place((i - y) % NY)) for i in range(NY)])

    total = (kl_sum + to_y(kl_sum, 2)) + (to_y(kl_sum, 1) + to_y(kl_sum, -1))
    loss = total[0, 0]
    return (loss / tokens, grad_hidden, grad_weight)


def solution(mesh):
    in_specs = (P(None, "hid"), P("hid", "vocab"), P(("vocab", "hid"), None))
    out_specs = (P(), P("vocab", "hid"), P("hid", "vocab"))
    return jax.shard_map(shards, mesh=mesh, in_specs=in_specs, out_specs=out_specs, check_vma=False)
```

```python
import jax
import jax.numpy as jnp
from jax import lax
from jax.experimental import pallas as pl
from jax.experimental.pallas import tpu as pltpu
from jax.sharding import PartitionSpec as P

BF16 = jnp.bfloat16
F32 = jnp.float32
NX, NZ, NY = 4, 8, 4
ORDER = (2, 1, 3, 0)


def to_core(a):
    return lax.ppermute(a, "hid", [(i, i ^ 1) for i in range(2 * NY)])


def to_y(a, d):
    return lax.ppermute(a, "hid", [(i, (i + 2 * d) % (2 * NY)) for i in range(2 * NY)])


def to_x(a, d):
    return lax.ppermute(a, "vocab", [(i, (i + NZ * d) % (NX * NZ)) for i in range(NX * NZ)])


def take(a, i):
    return lax.dynamic_index_in_dim(a, i, 0, keepdims=False)


def terms_kernel(logits_a, logits_b, teacher_ref, out_ref, table_ref):
    half = logits_a.shape[0]
    block = 32
    lane = lax.broadcasted_iota(jnp.int32, (block, 128), 1)

    def fill(logits_ref, start):
        def step(i, _):
            at = pl.multiple_of(i * block, block)
            logits = logits_ref[pl.ds(at, block)]
            teacher = teacher_ref[pl.ds(start + at, block)].astype(F32)
            m = jnp.max(logits, axis=1, keepdims=True)
            mt = jnp.max(teacher, axis=1, keepdims=True)
            ls = logits - m
            lt = teacher - mt
            e = jnp.exp(ls)
            s = jnp.sum(e, axis=1, keepdims=True)
            st = jnp.sum(jnp.exp(lt), axis=1, keepdims=True)
            cross = jnp.sum(e * (ls - lt), axis=1, keepdims=True)
            out = jnp.zeros((block, 128), F32)
            for k, column in enumerate((m, s, mt, st, cross)):
                out = jnp.where(lane == k, column, out)
            table_ref[pl.ds(start + at, block)] = out
            return 0

        lax.fori_loop(0, half // block, step, 0)

    fill(logits_a, 0)
    fill(logits_b, half)
    terms = table_ref[...].T[:8]

    def copy(i, _):
        out_ref[i] = terms
        return 0

    lax.fori_loop(0, out_ref.shape[0], copy, 0)


def row_terms(logits_a, logits_b, teacher, copies):
    rows, width = teacher.shape
    return pl.pallas_call(
        terms_kernel,
        out_shape=jax.ShapeDtypeStruct((copies, 8, rows), F32),
        scratch_shapes=[pltpu.VMEM((rows, 128), F32)],
        compiler_params=pltpu.CompilerParams(vmem_limit_bytes=24 * 2**20),
        cost_estimate=pl.CostEstimate(
            flops=12 * teacher.size,
            bytes_accessed=6 * teacher.size,
            transcendentals=2 * teacher.size,
        ),
    )(logits_a, logits_b, teacher)


def shards(student_hidden, head_weight, teacher_logits):
    n_vocab = NX * NZ
    tokens, depth = student_hidden.shape
    width = head_weight.shape[1]
    hid = lax.axis_index("hid")
    y, core = hid // 2, hid % 2
    x = lax.axis_index("vocab") // NZ
    rows = tokens // 8
    half = rows // 2

    def rows_of(hidden, part, *ds):
        by_part = take(hidden.reshape(2, 16, NY, 8, depth), core if part == 0 else 1 - core)
        return jnp.concatenate(
            [
                lax.dynamic_index_in_dim(by_part, (y + d) % NY, 1, keepdims=False).reshape(
                    rows, depth
                )
                for d in ds
            ]
        )

    def dot(a):
        return jnp.dot(a, head_weight, preferred_element_type=F32)

    def both_parts(*ds):
        return lax.optimization_barrier(
            (rows_of(student_hidden, 1, *ds), rows_of(student_hidden, 0, *ds))
        )

    h_far_b, h_far = both_parts(2)
    got = to_core(dot(h_far_b))
    far = dot(h_far) + got
    h_near_b, h_near = both_parts(1, 3)
    h_near_b, h_near, far = lax.optimization_barrier((h_near_b, h_near, far))
    r1 = to_y(far[:half], 1)
    r2 = to_y(far[half:], -1)
    got = to_core(dot(h_near_b))
    near = dot(h_near) + got
    r3 = to_y(near[half:rows], 1)
    r4 = to_y(near[rows : rows + half], -1)
    h_own_b, h_own = both_parts(0)
    h_own_b, h_own, near = lax.optimization_barrier((h_own_b, h_own, near))
    both = dot(jnp.concatenate([h_own_b, h_own]))
    own = both[rows:] + to_core(both[:rows])
    teacher_logits, _ = lax.optimization_barrier((teacher_logits, near))
    r1, r2, r3, r4, hidden_again = lax.optimization_barrier((r1, r2, r3, r4, student_hidden))
    tiles = lax.all_to_all(teacher_logits, "vocab", split_axis=1, concat_axis=0, tiled=True)
    tiles = tiles.reshape(2, 16, 4, width)
    theirs = to_core(take(tiles, 1 - core))
    both = jnp.stack([take(tiles, core), theirs])
    teacher = jnp.stack([take(both, core), take(both, 1 - core)], axis=1).reshape(rows, width)
    hiddens = jnp.concatenate(
        [rows_of(hidden_again, 0, *ORDER), rows_of(hidden_again, 1, *ORDER)]
    ).T
    teacher, hiddens = lax.optimization_barrier((teacher, hiddens))
    r5 = to_y(near[:half] + r1, 1)
    r6 = to_y(near[rows + half :] + r2, -1)
    logits = (own[:half] + (r4 + r5), own[half:] + (r3 + r6))

    terms = row_terms(*logits, teacher, n_vocab)
    terms = lax.all_to_all(terms, "vocab", split_axis=0, concat_axis=0, tiled=True)
    gm, gs, gmt, gst, gc = (terms[:, i] for i in range(5))
    top, top_t = jnp.max(gm, axis=0), jnp.max(gmt, axis=0)
    w = jnp.exp(gm - top)
    total = jnp.sum(gs * w, axis=0)
    total_t = jnp.sum(gst * jnp.exp(gmt - top_t), axis=0)
    log_total, log_total_t = jnp.log(total), jnp.log(total_t)
    mean_ratio = jnp.sum(w * (gc + gs * ((gm - top) - (gmt - top_t))), axis=0) / total
    kl_row = mean_ratio - log_total + log_total_t
    lse = top + log_total
    lse_t = top_t + log_total_t

    student_log = jnp.concatenate(logits) - lse[:, None]
    teacher_log = teacher.astype(F32) - lse_t[:, None]
    probs = jnp.exp(student_log)
    grad = (probs * (student_log - teacher_log - kl_row[:, None]) / tokens).astype(BF16)

    g1, g2 = grad[:half], grad[half:]
    a1, a2 = to_y(g1, 1), to_y(g2, -1)
    own_b = to_core(grad)
    a3, a4 = to_y(g2, 1), to_y(g1, -1)
    a5, a6 = to_y(a1, 1), to_y(a2, -1)
    near = jnp.concatenate([a4, a2, a1, a3])
    near_b = to_core(near)
    far = jnp.concatenate([a5, a6])
    far_b = to_core(far)

    grads = jnp.concatenate([far, near, grad, far_b, near_b, own_b])
    part_hidden = lax.dot_general(
        grads, head_weight, (((1,), (1,)), ((), ())), preferred_element_type=F32
    ).astype(BF16)
    part_hidden = part_hidden.reshape(2, NY, 2, NZ, 8, depth)

    def for_x(d):
        to = (x + d) % NX
        which = jnp.where(to // 2 == core, 0, 1)
        piece = lax.dynamic_slice(
            part_hidden, (which, 0, to % 2, 0, 0, 0), (1, NY, 1, NZ, 8, depth)
        )
        return piece.reshape(NY, NZ, 8, depth)

    got = [to_x(for_x(d), d) for d in (2, 1, 3)]
    summed = sum((g.astype(F32) for g in got), for_x(0).astype(F32))
    summed = summed.astype(BF16)
    grad_weight = jnp.dot(hiddens, grads, preferred_element_type=F32).astype(BF16)

    summed, grad_weight, kl_row = lax.optimization_barrier((summed, grad_weight, kl_row))
    kl_sum = jnp.broadcast_to(jnp.sum(kl_row), (8, 128))
    kl_sum = kl_sum + to_core(kl_sum)
    summed = summed.transpose(1, 0, 2, 3).reshape(NZ * NY * 8, depth)
    z_groups = [[i * NZ + j for j in range(NZ)] for i in range(NX)]
    pieces = lax.all_to_all(
        summed, "vocab", split_axis=0, concat_axis=0, tiled=True, axis_index_groups=z_groups
    )
    rel = jnp.sum(pieces.reshape(NZ, NY, 8, depth).astype(F32), axis=0).astype(BF16)
    def place(d):
        return jnp.where(d == 2, 0, jnp.where(d == 0, 3, jnp.where(d == 1, 1, 2)))

    grad_hidden = jnp.concatenate([take(rel, place((i - y) % NY)) for i in range(NY)])

    total = (kl_sum + to_y(kl_sum, 2)) + (to_y(kl_sum, 1) + to_y(kl_sum, -1))
    loss = total[0, 0]
    return (loss / tokens, grad_hidden, grad_weight)


def solution(mesh):
    in_specs = (P(None, "hid"), P("hid", "vocab"), P(("vocab", "hid"), None))
    out_specs = (P(), P("vocab", "hid"), P("hid", "vocab"))
    return jax.shard_map(shards, mesh=mesh, in_specs=in_specs, out_specs=out_specs, check_vma=False)
```

```python
import jax
import jax.numpy as jnp
from jax import lax
from jax.experimental import pallas as pl
from jax.experimental.pallas import tpu as pltpu
from jax.sharding import PartitionSpec as P

BF16 = jnp.bfloat16
F32 = jnp.float32
NX, NZ, NY = 4, 8, 4
ORDER = (2, 1, 3, 0)


def to_core(a):
    return lax.ppermute(a, "hid", [(i, i ^ 1) for i in range(2 * NY)])


def to_y(a, d):
    return lax.ppermute(a, "hid", [(i, (i + 2 * d) % (2 * NY)) for i in range(2 * NY)])


def to_x(a, d):
    return lax.ppermute(a, "vocab", [(i, (i + NZ * d) % (NX * NZ)) for i in range(NX * NZ)])


def take(a, i):
    return lax.dynamic_index_in_dim(a, i, 0, keepdims=False)


def terms_kernel(logits_a, logits_b, teacher_ref, out_ref):
    half = logits_a.shape[0]
    rows = 2 * half
    lane = lax.broadcasted_iota(jnp.int32, (half, 128), 1)

    def table(logits, teacher):
        m = jnp.max(logits, axis=1, keepdims=True)
        mt = jnp.max(teacher, axis=1, keepdims=True)
        ls = logits - m
        lt = teacher - mt
        e = jnp.exp(ls)
        s = jnp.sum(e, axis=1, keepdims=True)
        st = jnp.sum(jnp.exp(lt), axis=1, keepdims=True)
        cross = jnp.sum(e * (ls - lt), axis=1, keepdims=True)
        out = jnp.zeros((half, 128), F32)
        for i, column in enumerate((m, s, mt, st, cross)):
            out = jnp.where(lane == i, column, out)
        return out

    terms = jnp.concatenate(
        [
            table(logits_a[...], teacher_ref[:half].astype(F32)),
            table(logits_b[...], teacher_ref[half:].astype(F32)),
        ]
    ).T[:8]
    for i in range(out_ref.shape[0]):
        out_ref[i] = terms


def row_terms(logits_a, logits_b, teacher, copies):
    rows, width = teacher.shape
    return pl.pallas_call(
        terms_kernel,
        out_shape=jax.ShapeDtypeStruct((copies, 8, rows), F32),
        compiler_params=pltpu.CompilerParams(vmem_limit_bytes=24 * 2**20),
        cost_estimate=pl.CostEstimate(
            flops=12 * teacher.size,
            bytes_accessed=6 * teacher.size,
            transcendentals=2 * teacher.size,
        ),
    )(logits_a, logits_b, teacher)


def shards(student_hidden, head_weight, teacher_logits):
    n_vocab = NX * NZ
    tokens, depth = student_hidden.shape
    width = head_weight.shape[1]
    hid = lax.axis_index("hid")
    y, core = hid // 2, hid % 2
    x = lax.axis_index("vocab") // NZ
    rows = tokens // 8
    half = rows // 2

    def rows_of(hidden, part, *ds):
        by_part = take(hidden.reshape(2, 16, NY, 8, depth), core if part == 0 else 1 - core)
        return jnp.concatenate(
            [
                lax.dynamic_index_in_dim(by_part, (y + d) % NY, 1, keepdims=False).reshape(
                    rows, depth
                )
                for d in ds
            ]
        )

    def dot(a):
        return jnp.dot(a, head_weight, preferred_element_type=F32)

    def both_parts(*ds):
        return lax.optimization_barrier(
            (rows_of(student_hidden, 1, *ds), rows_of(student_hidden, 0, *ds))
        )

    h_far_b, h_far = both_parts(2)
    got = to_core(dot(h_far_b))
    far = dot(h_far) + got
    h_near_b, h_near = both_parts(1, 3)
    h_near_b, h_near, far = lax.optimization_barrier((h_near_b, h_near, far))
    r1 = to_y(far[:half], 1)
    r2 = to_y(far[half:], -1)
    got = to_core(dot(h_near_b))
    near = dot(h_near) + got
    r3 = to_y(near[half:rows], 1)
    r4 = to_y(near[rows : rows + half], -1)
    h_own_b, h_own = both_parts(0)
    h_own_b, h_own, near = lax.optimization_barrier((h_own_b, h_own, near))
    both = dot(jnp.concatenate([h_own_b, h_own]))
    own = both[rows:] + to_core(both[:rows])
    teacher_logits, _ = lax.optimization_barrier((teacher_logits, near))
    r1, r2, r3, r4, hidden_again = lax.optimization_barrier((r1, r2, r3, r4, student_hidden))
    tiles = lax.all_to_all(teacher_logits, "vocab", split_axis=1, concat_axis=0, tiled=True)
    tiles = tiles.reshape(2, 16, 4, width)
    theirs = to_core(take(tiles, 1 - core))
    both = jnp.stack([take(tiles, core), theirs])
    teacher = jnp.stack([take(both, core), take(both, 1 - core)], axis=1).reshape(rows, width)
    hiddens = jnp.concatenate(
        [rows_of(hidden_again, 0, *ORDER), rows_of(hidden_again, 1, *ORDER)]
    ).T
    teacher, hiddens = lax.optimization_barrier((teacher, hiddens))
    r5 = to_y(near[:half] + r1, 1)
    r6 = to_y(near[rows + half :] + r2, -1)
    logits = (own[:half] + (r4 + r5), own[half:] + (r3 + r6))

    terms = row_terms(*logits, teacher, n_vocab)
    terms = lax.all_to_all(terms, "vocab", split_axis=0, concat_axis=0, tiled=True)
    gm, gs, gmt, gst, gc = (terms[:, i] for i in range(5))
    top, top_t = jnp.max(gm, axis=0), jnp.max(gmt, axis=0)
    w = jnp.exp(gm - top)
    total = jnp.sum(gs * w, axis=0)
    total_t = jnp.sum(gst * jnp.exp(gmt - top_t), axis=0)
    log_total, log_total_t = jnp.log(total), jnp.log(total_t)
    mean_ratio = jnp.sum(w * (gc + gs * ((gm - top) - (gmt - top_t))), axis=0) / total
    kl_row = mean_ratio - log_total + log_total_t
    lse = top + log_total
    lse_t = top_t + log_total_t

    student_log = jnp.concatenate(logits) - lse[:, None]
    teacher_log = teacher.astype(F32) - lse_t[:, None]
    probs = jnp.exp(student_log)
    grad = (probs * (student_log - teacher_log - kl_row[:, None]) / tokens).astype(BF16)

    g1, g2 = grad[:half], grad[half:]
    a1, a2 = to_y(g1, 1), to_y(g2, -1)
    own_b = to_core(grad)
    a3, a4 = to_y(g2, 1), to_y(g1, -1)
    a5, a6 = to_y(a1, 1), to_y(a2, -1)
    near = jnp.concatenate([a4, a2, a1, a3])
    near_b = to_core(near)
    far = jnp.concatenate([a5, a6])
    far_b = to_core(far)

    grads = jnp.concatenate([far, near, grad, far_b, near_b, own_b])
    part_hidden = lax.dot_general(
        grads, head_weight, (((1,), (1,)), ((), ())), preferred_element_type=F32
    ).astype(BF16)
    part_hidden = part_hidden.reshape(2, NY, 2, NZ, 8, depth)

    def for_x(d):
        to = (x + d) % NX
        which = jnp.where(to // 2 == core, 0, 1)
        piece = lax.dynamic_slice(
            part_hidden, (which, 0, to % 2, 0, 0, 0), (1, NY, 1, NZ, 8, depth)
        )
        return piece.reshape(NY, NZ, 8, depth)

    got = [to_x(for_x(d), d) for d in (2, 1, 3)]
    summed = sum((g.astype(F32) for g in got), for_x(0).astype(F32))
    summed = summed.astype(BF16)
    grad_weight = jnp.dot(hiddens, grads, preferred_element_type=F32).astype(BF16)

    summed, grad_weight, kl_row = lax.optimization_barrier((summed, grad_weight, kl_row))
    kl_sum = jnp.broadcast_to(jnp.sum(kl_row), (8, 128))
    kl_sum = kl_sum + to_core(kl_sum)
    summed = summed.transpose(1, 0, 2, 3).reshape(NZ * NY * 8, depth)
    z_groups = [[i * NZ + j for j in range(NZ)] for i in range(NX)]
    pieces = lax.all_to_all(
        summed, "vocab", split_axis=0, concat_axis=0, tiled=True, axis_index_groups=z_groups
    )
    rel = jnp.sum(pieces.reshape(NZ, NY, 8, depth).astype(F32), axis=0).astype(BF16)
    def place(d):
        return jnp.where(d == 2, 0, jnp.where(d == 0, 3, jnp.where(d == 1, 1, 2)))

    grad_hidden = jnp.concatenate([take(rel, place((i - y) % NY)) for i in range(NY)])

    total = (kl_sum + to_y(kl_sum, 2)) + (to_y(kl_sum, 1) + to_y(kl_sum, -1))
    loss = total[0, 0]
    return (loss / tokens, grad_hidden, grad_weight)


def solution(mesh):
    in_specs = (P(None, "hid"), P("hid", "vocab"), P(("vocab", "hid"), None))
    out_specs = (P(), P("vocab", "hid"), P("hid", "vocab"))
    return jax.shard_map(shards, mesh=mesh, in_specs=in_specs, out_specs=out_specs, check_vma=False)
```
